512 devices in a mesh: dp: 64 (over y, x, z_hi), tensor: 8 (over z_lo, core).
Axes of the slice: x: 4, y: 4, z: 16 (z_hi: 4, z_lo: 4; z = z_hi * 4 + z_lo), core: 2. Of those that a mesh axis runs over, the one named last changes fastest.
Arguments:
- inputs: bfloat16 [384, 16384], P('tensor', 'dp'), may hold values from -6 to 6
- out_grad: bfloat16 [384, 16384], P('tensor', 'dp'), may hold values from -6 to 6
- gate_weight: bfloat16 [16384, 8192], P('dp', 'tensor'), may hold values from -0.046875 to 0.046875
- up_weight: bfloat16 [16384, 8192], P('dp', 'tensor'), may hold values from -0.046875 to 0.046875
- down_weight: bfloat16 [8192, 16384], P('tensor', 'dp'), may hold values from -0.0625 to 0.0625
- segment_ids: int32 [384], P('tensor'), may hold values from 0 to 7, never falling along the last dimension, each value on 1 to 96 neighbouring positions
- token_weights: int32 [384], P('tensor'), may hold values from 1 to 16
Outputs:
- grad_gate: bfloat16 [16384, 8192], P('dp', 'tensor')
- grad_up: bfloat16 [16384, 8192], P('dp', 'tensor')
- grad_down: bfloat16 [8192, 16384], P('tensor', 'dp')
- grad_input: bfloat16 [384, 16384], P('tensor', 'dp')
The draws below stay inside these ranges and needn't reach their ends.
Inputs may be any that keep to these rules, and one draw needn't show every extreme that they name: `segment_ids`: ids never fall along the tokens; each document holds 1 to 96 tokens.
All inputs are finite; a program needn't handle non-finite values.
Results may differ from the reference program's by a relative error of at most 0.0057.
Values may be sent and summed in bfloat16 or wider, within the bound.
No kernel may reach another device: no remote copies, remote signals or barrier semaphores. Data moves between devices by JAX's collectives and lax.ppermute only.
A program may use at most 64 MiB of HBM per device.

```python
import math
import jax
import jax.numpy as jnp
import numpy as np
from jax import lax

D = 16384
FF = 8192
TOKENS = 384
SEGMENTS = 8


def set_ends(values, rng, low, high):
    dims = values.shape
    place = [jax.random.randint(jax.random.fold_in(rng, axis), (), 0, dims[axis]) for axis in range(len(dims))]
    values = values.at[tuple(place)].set(low)
    longest = dims.index(max(dims))
    place[longest] = (place[longest] + 1) % dims[longest]
    return values.at[tuple(place)].set(high)


def block_scale(own_key, shape, shards, least, high):
    def one(axis_at, blocks):
        heights = jax.random.uniform(jax.random.fold_in(jax.random.fold_in(own_key, 6), axis_at), (blocks,), jnp.float32, least / len(shards), high / len(shards))
        return jnp.repeat(jnp.exp(heights), shape[axis_at] // blocks).reshape((-1,) + (1,) * (len(shape) - axis_at - 1))

    loudness = one(*shards[0])
    for cut in shards[1:]:
        loudness = loudness * one(*cut)
    return loudness


def split_up(number_of, total, limit, slope):
    loads = [(1 << 20) // math.isqrt(grade ** slope) + 1 for grade in range(2, number_of + 1)]
    rest, counts = total - limit - (number_of - 1), [1] * (number_of - 1)
    while rest > 0:
        candidates = [i for i in range(number_of - 1) if counts[i] < limit]
        pool, remaining = sum([loads[i] for i in candidates]), rest
        for i in candidates:
            addition = min(limit - counts[i], max(1, remaining * loads[i] // pool), rest)
            counts[i] = counts[i] + addition
            rest = rest - addition
    return np.array([limit] + counts)


def ragged(rng, number_of, total, limit, skew):
    if number_of == 2:
        one = jax.random.randint(rng, (), max(1, total - limit), min(limit, total - 1) + 1)
        return jnp.stack([one, total - one])
    sizes = jnp.asarray(split_up(number_of, total, limit, skew), jnp.int32)
    twos = (number_of - 1) // 2
    source_of, sink = sizes[1:1 + 2 * twos:2], sizes[2:2 + 2 * twos:2]
    room = jnp.minimum(source_of - 1, limit - sink)
    passed = jax.random.randint(jax.random.fold_in(rng, 1), (twos,), 0, 1 << 20) % (room + 1)
    sizes = sizes.at[1:1 + 2 * twos:2].set(source_of - passed).at[2:2 + 2 * twos:2].set(sink + passed)
    return sizes[jax.random.permutation(jax.random.fold_in(rng, 2), number_of)]


def scatter_about(own_key, dims, deviation, bound, pieces=(), kind=jnp.bfloat16):
    factor_of = block_scale(own_key, dims, pieces, -0.22, 0.18) if pieces else 1.0
    values = jax.random.normal(own_key, dims, jnp.float32) * deviation * factor_of
    return jnp.minimum(jnp.maximum(values, -bound), bound).astype(kind)


def setup_inputs(seed: int = 0) -> dict:
    key_list = jax.random.split(jax.random.key(seed), 8)
    return {
        "inputs": scatter_about(key_list[0], (TOKENS, D), 1.0, 6.0, ((0, 8), (1, 64))),
        "out_grad": scatter_about(key_list[1], (TOKENS, D), 1.0, 6.0, ((0, 8), (1, 64))),
        "gate_weight": scatter_about(key_list[2], (D, FF), D ** -0.5, 0.046875, ((0, 64), (1, 8))),
        "up_weight": scatter_about(key_list[3], (D, FF), D ** -0.5, 0.046875, ((0, 64), (1, 8))),
        "down_weight": scatter_about(key_list[4], (FF, D), FF ** -0.5, 0.0625, ((0, 8), (1, 64))),
        "segment_ids": jnp.searchsorted(jnp.cumsum(ragged(key_list[5], SEGMENTS, TOKENS, TOKENS // 4, 1)), jnp.arange(TOKENS), side="right").astype(jnp.int32),
        "token_weights": set_ends(jax.random.randint(key_list[6], (TOKENS,), 1, 17), jax.random.fold_in(key_list[6], 1), 1, 16).astype(jnp.int32),
    }


def token_scale(segment_ids, token_weights):
    same = segment_ids[:, None] == segment_ids[None, :]
    seg_total = jnp.sum(jnp.where(same, token_weights[None, :], 0), axis=1)
    seg_count = jnp.sum(same.astype(jnp.int32), axis=1)
    return (token_weights * seg_count).astype(jnp.float32) / seg_total.astype(jnp.float32)


def reference(inputs, out_grad, gate_weight, up_weight, down_weight, segment_ids, token_weights):
    gate = jnp.dot(inputs, gate_weight, preferred_element_type=jnp.float32)
    up = jnp.dot(inputs, up_weight, preferred_element_type=jnp.float32)
    sigma = jax.nn.sigmoid(gate)
    hidden = (gate * sigma * up).astype(jnp.bfloat16)
    scale = token_scale(segment_ids, token_weights)
    weighted = (out_grad.astype(jnp.float32) * scale[:, None]).astype(jnp.bfloat16)
    hidden_grad = lax.dot_general(weighted, down_weight, (((1,), (1,)), ((), ())), preferred_element_type=jnp.float32)
    gate_grad = (hidden_grad * up * sigma * (1.0 + gate * (1.0 - sigma))).astype(jnp.bfloat16)
    up_grad = (hidden_grad * gate * sigma).astype(jnp.bfloat16)
    grad_down = lax.dot_general(hidden, weighted, (((0,), (0,)), ((), ())), preferred_element_type=jnp.float32).astype(jnp.bfloat16)
    grad_gate = lax.dot_general(inputs, gate_grad, (((0,), (0,)), ((), ())), preferred_element_type=jnp.float32).astype(jnp.bfloat16)
    grad_up = lax.dot_general(inputs, up_grad, (((0,), (0,)), ((), ())), preferred_element_type=jnp.float32).astype(jnp.bfloat16)
    back = lax.dot_general(gate_grad, gate_weight, (((1,), (1,)), ((), ())), preferred_element_type=jnp.float32)
    back = back + lax.dot_general(up_grad, up_weight, (((1,), (1,)), ((), ())), preferred_element_type=jnp.float32)
    return grad_gate, grad_up, grad_down, back.astype(jnp.bfloat16)
```

```python
import jax
import jax.numpy as jnp
from jax import lax
from jax.sharding import Mesh, PartitionSpec as P

YX = ("y", "x")
TENSOR = ("zl", "c")
TOKENS = 384
FF = 1024


def contract(left, right, dims):
    return lax.dot_general(left, right, (dims, ((), ())), preferred_element_type=jnp.float32)


def token_scale(ids, weights):
    same = ids[:, None] == ids[None, :]
    total = jnp.sum(jnp.where(same, weights[None, :], 0.0), axis=1)
    count = jnp.sum(same.astype(jnp.float32), axis=1)
    return weights * count / total


def derivatives(sums):
    gate, up, hidden_grad = jnp.split(sums, 3, axis=-1)
    sigma = jax.nn.sigmoid(gate)
    hidden = gate * sigma * up
    gate_grad = hidden_grad * up * sigma * (1.0 + gate * (1.0 - sigma))
    up_grad = hidden_grad * gate * sigma
    return jnp.concatenate([hidden, gate_grad, up_grad], axis=-1).astype(jnp.bfloat16)


def shards(inputs, out_grad, gate_weight, up_weight, down_weight, segment_ids, token_weights):
    side = jnp.stack([segment_ids, token_weights], axis=1).astype(jnp.bfloat16)
    side = jnp.pad(side, ((0, 0), (0, 126)))
    own = jnp.concatenate([inputs, out_grad, side], axis=1)
    every = lax.all_gather(own, TENSOR, axis=0, tiled=True)
    all_inputs, all_grads = every[:, :256], every[:, 256:512]
    scale = token_scale(every[:, 512].astype(jnp.float32), every[:, 513].astype(jnp.float32))
    weighted = (all_grads.astype(jnp.float32) * scale[:, None]).astype(jnp.bfloat16)

    parts = jnp.concatenate(
        [
            contract(all_inputs, gate_weight, ((1,), (0,))).astype(jnp.bfloat16),
            contract(all_inputs, up_weight, ((1,), (0,))).astype(jnp.bfloat16),
            contract(weighted, down_weight, ((1,), (1,))).astype(jnp.bfloat16),
        ],
        axis=1,
    )
    pieces = lax.all_to_all(parts.reshape(16, TOKENS // 16, 3 * FF), YX, 0, 0)
    partial = jnp.sum(pieces.astype(jnp.float32), axis=0).astype(jnp.bfloat16)
    partials = lax.all_gather(partial, "zh", axis=0)
    own_block = derivatives(jnp.sum(partials.astype(jnp.float32), axis=0))
    blocks = lax.all_to_all(jnp.broadcast_to(own_block[None], (16,) + own_block.shape), YX, 0, 0)
    blocks = blocks.reshape(TOKENS, 3 * FF)
    hidden, gate_grad, up_grad = blocks[:, :FF], blocks[:, FF : 2 * FF], blocks[:, 2 * FF :]

    back = contract(gate_grad, gate_weight, ((1,), (1,))) + contract(up_grad, up_weight, ((1,), (1,)))
    back = lax.all_to_all(back.reshape(8, TOKENS // 8, 256), TENSOR, 0, 0)
    grad_input = jnp.sum(back, axis=0).astype(jnp.bfloat16)
    grad_gate = contract(all_inputs, gate_grad, ((0,), (0,))).astype(jnp.bfloat16)
    grad_up = contract(all_inputs, up_grad, ((0,), (0,))).astype(jnp.bfloat16)
    grad_down = contract(hidden, weighted, ((0,), (0,))).astype(jnp.bfloat16)
    return grad_gate, grad_up, grad_down, grad_input


def solution(mesh):
    fine = Mesh(mesh.devices.reshape(4, 4, 4, 4, 2), ("y", "x", "zh", "zl", "c"))
    dp = ("y", "x", "zh")
    in_specs = (
        P(TENSOR, dp),
        P(TENSOR, dp),
        P(dp, TENSOR),
        P(dp, TENSOR),
        P(TENSOR, dp),
        P(TENSOR),
        P(TENSOR),
    )
    out_specs = (P(dp, TENSOR), P(dp, TENSOR), P(TENSOR, dp), P(TENSOR, dp))
    return jax.shard_map(shards, mesh=fine, in_specs=in_specs, out_specs=out_specs, check_vma=False)
```

```python
import jax
import jax.numpy as jnp
from jax import lax
from jax.sharding import Mesh, PartitionSpec as P

YX = ("y", "x")
TENSOR = ("zl", "c")
TOKENS = 384
FF = 1024


def contract(left, right, dims):
    return lax.dot_general(left, right, (dims, ((), ())), preferred_element_type=jnp.float32)


def token_scale(ids, weights):
    same = ids[:, None] == ids[None, :]
    total = jnp.sum(jnp.where(same, weights[None, :], 0.0), axis=1)
    count = jnp.sum(same.astype(jnp.float32), axis=1)
    return weights * count / total


def derivatives(sums):
    gate, up, hidden_grad = jnp.split(sums, 3, axis=-1)
    sigma = jax.nn.sigmoid(gate)
    hidden = gate * sigma * up
    gate_grad = hidden_grad * up * sigma * (1.0 + gate * (1.0 - sigma))
    up_grad = hidden_grad * gate * sigma
    return jnp.concatenate([hidden, gate_grad, up_grad], axis=-1).astype(jnp.bfloat16)


def shards(inputs, out_grad, gate_weight, up_weight, down_weight, segment_ids, token_weights):
    side = jnp.stack([segment_ids, token_weights], axis=1).astype(jnp.bfloat16)
    side = jnp.pad(side, ((0, 0), (0, 126)))
    own = jnp.concatenate([inputs, out_grad, side], axis=1)
    every = lax.all_gather(own, TENSOR, axis=0, tiled=True)
    all_inputs, all_grads = every[:, :256], every[:, 256:512]
    scale = token_scale(every[:, 512].astype(jnp.float32), every[:, 513].astype(jnp.float32))
    weighted = (all_grads.astype(jnp.float32) * scale[:, None]).astype(jnp.bfloat16)

    parts = jnp.concatenate(
        [
            contract(all_inputs, gate_weight, ((1,), (0,))).astype(jnp.bfloat16),
            contract(all_inputs, up_weight, ((1,), (0,))).astype(jnp.bfloat16),
            contract(weighted, down_weight, ((1,), (1,))).astype(jnp.bfloat16),
        ],
        axis=1,
    )
    pieces = lax.all_to_all(parts.reshape(16, TOKENS // 16, 3 * FF), YX, 0, 0)
    partial = jnp.sum(pieces.astype(jnp.float32), axis=0).astype(jnp.bfloat16)
    partials = lax.all_gather(partial, "zh", axis=0)
    own_block = derivatives(jnp.sum(partials.astype(jnp.float32), axis=0))
    blocks = lax.all_to_all(jnp.broadcast_to(own_block[None], (16,) + own_block.shape), YX, 0, 0)
    blocks = blocks.reshape(TOKENS, 3 * FF)
    hidden, gate_grad, up_grad = blocks[:, :FF], blocks[:, FF : 2 * FF], blocks[:, 2 * FF :]

    back = contract(gate_grad, gate_weight, ((1,), (1,))) + contract(up_grad, up_weight, ((1,), (1,)))
    back = lax.all_to_all(back.astype(jnp.bfloat16).reshape(8, TOKENS // 8, 256), TENSOR, 0, 0)
    grad_input = jnp.sum(back.astype(jnp.float32), axis=0).astype(jnp.bfloat16)
    grad_gate = contract(all_inputs, gate_grad, ((0,), (0,))).astype(jnp.bfloat16)
    grad_up = contract(all_inputs, up_grad, ((0,), (0,))).astype(jnp.bfloat16)
    grad_down = contract(hidden, weighted, ((0,), (0,))).astype(jnp.bfloat16)
    return grad_gate, grad_up, grad_down, grad_input


def solution(mesh):
    fine = Mesh(mesh.devices.reshape(4, 4, 4, 4, 2), ("y", "x", "zh", "zl", "c"))
    dp = ("y", "x", "zh")
    in_specs = (
        P(TENSOR, dp),
        P(TENSOR, dp),
        P(dp, TENSOR),
        P(dp, TENSOR),
        P(TENSOR, dp),
        P(TENSOR),
        P(TENSOR),
    )
    out_specs = (P(dp, TENSOR), P(dp, TENSOR), P(TENSOR, dp), P(TENSOR, dp))
    return jax.shard_map(shards, mesh=fine, in_specs=in_specs, out_specs=out_specs, check_vma=False)
```

```python
import jax
import jax.numpy as jnp
from jax import lax
from jax.sharding import Mesh, PartitionSpec as P

YX = ("x", "y")
TENSOR = ("zm", "zl", "c")
TOKENS = 384
FF = 1024


def contract(left, right, dims):
    return lax.dot_general(left, right, (dims, ((), ())), preferred_element_type=jnp.float32)


def token_scale(ids, weights):
    same = ids[:, None] == ids[None, :]
    total = jnp.sum(jnp.where(same, weights[None, :], 0.0), axis=1)
    count = jnp.sum(same.astype(jnp.float32), axis=1)
    return weights * count / total


def derivatives(sums):
    gate, up, hidden_grad = jnp.split(sums, 3, axis=-1)
    sigma = jax.nn.sigmoid(gate)
    hidden = gate * sigma * up
    gate_grad = hidden_grad * up * sigma * (1.0 + gate * (1.0 - sigma))
    up_grad = hidden_grad * gate * sigma
    return jnp.concatenate([hidden, gate_grad, up_grad], axis=-1).astype(jnp.bfloat16)


def shards(inputs, out_grad, gate_weight, up_weight, down_weight, segment_ids, token_weights):
    side = jnp.stack([segment_ids, token_weights], axis=1).astype(jnp.bfloat16)
    side = jnp.pad(side, ((0, 0), (0, 126)))
    own = jnp.concatenate([inputs, out_grad, side], axis=1)
    every = lax.all_gather(own, TENSOR, axis=0, tiled=True)
    all_inputs, all_grads = every[:, :256], every[:, 256:512]
    scale = token_scale(every[:, 512].astype(jnp.float32), every[:, 513].astype(jnp.float32))
    weighted = (all_grads.astype(jnp.float32) * scale[:, None]).astype(jnp.bfloat16)

    parts = jnp.concatenate(
        [
            contract(all_inputs, gate_weight, ((1,), (0,))).astype(jnp.bfloat16),
            contract(all_inputs, up_weight, ((1,), (0,))).astype(jnp.bfloat16),
            contract(weighted, down_weight, ((1,), (1,))).astype(jnp.bfloat16),
        ],
        axis=1,
    )
    parts, weighted, all_inputs = lax.optimization_barrier((parts, weighted, all_inputs))
    pieces = lax.all_to_all(parts.reshape(16, TOKENS // 16, 3 * FF), YX, 0, 0)
    partial = jnp.sum(pieces.astype(jnp.float32), axis=0).astype(jnp.bfloat16)
    partials = lax.all_gather(partial, "zh", axis=0)
    own_block = derivatives(jnp.sum(partials.astype(jnp.float32), axis=0))
    blocks = lax.all_to_all(jnp.broadcast_to(own_block[None], (16,) + own_block.shape), YX, 0, 0)
    blocks = blocks.reshape(TOKENS, 3 * FF)
    hidden, gate_grad, up_grad = blocks[:, :FF], blocks[:, FF : 2 * FF], blocks[:, 2 * FF :]

    back = contract(gate_grad, gate_weight, ((1,), (1,))) + contract(up_grad, up_weight, ((1,), (1,)))
    back = back.astype(jnp.bfloat16).reshape(2, 2, 2, TOKENS // 8, 256).swapaxes(0, 1).reshape(8, TOKENS // 8, 256)
    back = lax.all_to_all(back, ("zl", "zm", "c"), 0, 0)
    grad_input = jnp.sum(back.astype(jnp.float32), axis=0).astype(jnp.bfloat16)
    grad_gate = contract(all_inputs, gate_grad, ((0,), (0,))).astype(jnp.bfloat16)
    grad_up = contract(all_inputs, up_grad, ((0,), (0,))).astype(jnp.bfloat16)
    grad_down = contract(hidden, weighted, ((0,), (0,))).astype(jnp.bfloat16)
    return grad_gate, grad_up, grad_down, grad_input


def solution(mesh):
    fine = Mesh(mesh.devices.reshape(4, 4, 4, 2, 2, 2), ("y", "x", "zh", "zm", "zl", "c"))
    dp = ("y", "x", "zh")
    in_specs = (
        P(TENSOR, dp),
        P(TENSOR, dp),
        P(dp, TENSOR),
        P(dp, TENSOR),
        P(TENSOR, dp),
        P(TENSOR),
        P(TENSOR),
    )
    out_specs = (P(dp, TENSOR), P(dp, TENSOR), P(TENSOR, dp), P(TENSOR, dp))
    return jax.shard_map(shards, mesh=fine, in_specs=in_specs, out_specs=out_specs, check_vma=False)
```

```python
import jax
import jax.numpy as jnp
from jax import lax
from jax.sharding import Mesh, PartitionSpec as P

YX = ("x", "y")
TENSOR = ("zm", "zl", "c")
TOKENS = 384
FF = 1024


def contract(left, right, dims):
    return lax.dot_general(left, right, (dims, ((), ())), preferred_element_type=jnp.float32)


def token_scale(ids, weights):
    same = ids[:, None] == ids[None, :]
    total = jnp.sum(jnp.where(same, weights[None, :], 0.0), axis=1)
    count = jnp.sum(same.astype(jnp.float32), axis=1)
    return weights * count / total


def derivatives(sums):
    gate, up, hidden_grad = jnp.split(sums, 3, axis=-1)
    sigma = jax.nn.sigmoid(gate)
    hidden = gate * sigma * up
    gate_grad = hidden_grad * up * sigma * (1.0 + gate * (1.0 - sigma))
    up_grad = hidden_grad * gate * sigma
    return jnp.concatenate([hidden, gate_grad, up_grad], axis=-1).astype(jnp.bfloat16)


def shards(inputs, out_grad, gate_weight, up_weight, down_weight, segment_ids, token_weights):
    token = lax.broadcasted_iota(jnp.int32, (TOKENS // 8, 128), 0)
    lane = lax.broadcasted_iota(jnp.int32, (TOKENS // 8, 128), 1)
    codes = jnp.pad(segment_ids, (0, 80)) + jnp.pad(token_weights, (64, 16))
    side = jnp.where((lane & 63) == token, codes[None, :], 0).astype(jnp.bfloat16)
    own = jnp.concatenate([inputs, out_grad, side], axis=1)
    every = lax.all_gather(own, TENSOR, axis=0, tiled=True)
    all_inputs, all_grads = every[:, :256], every[:, 256:512]
    sides = every[:, 512:].astype(jnp.float32)
    scale = token_scale(jnp.sum(sides[:, :64], axis=1), jnp.sum(sides[:, 64:], axis=1))
    weighted = (all_grads.astype(jnp.float32) * scale[:, None]).astype(jnp.bfloat16)

    parts = jnp.concatenate(
        [
            contract(all_inputs, gate_weight, ((1,), (0,))).astype(jnp.bfloat16),
            contract(all_inputs, up_weight, ((1,), (0,))).astype(jnp.bfloat16),
            contract(weighted, down_weight, ((1,), (1,))).astype(jnp.bfloat16),
        ],
        axis=1,
    )
    parts, weighted, all_inputs = lax.optimization_barrier((parts, weighted, all_inputs))
    pieces = lax.all_to_all(parts.reshape(16, TOKENS // 16, 3 * FF), YX, 0, 0)
    own_sum = jnp.sum(pieces.astype(jnp.float32), axis=0)
    rounded = lax.reduce_precision(own_sum, 8, 7)
    partials = lax.all_gather(rounded.astype(jnp.bfloat16), "zh", axis=0)
    own_block = derivatives(jnp.sum(partials.astype(jnp.float32), axis=0) + (own_sum - rounded))
    blocks = lax.all_to_all(jnp.broadcast_to(own_block[None], (16,) + own_block.shape), YX, 0, 0)
    blocks = blocks.reshape(TOKENS, 3 * FF)
    hidden, gate_grad, up_grad = blocks[:, :FF], blocks[:, FF : 2 * FF], blocks[:, 2 * FF :]

    back = contract(gate_grad, gate_weight, ((1,), (1,))) + contract(up_grad, up_weight, ((1,), (1,)))
    back = back.astype(jnp.bfloat16).reshape(2, 2, 2, TOKENS // 8, 256).swapaxes(0, 1).reshape(8, TOKENS // 8, 256)
    back = lax.all_to_all(back, ("zl", "zm", "c"), 0, 0)
    grad_input = jnp.sum(back.astype(jnp.float32), axis=0).astype(jnp.bfloat16)
    grad_gate = contract(all_inputs, gate_grad, ((0,), (0,))).astype(jnp.bfloat16)
    grad_up = contract(all_inputs, up_grad, ((0,), (0,))).astype(jnp.bfloat16)
    grad_down = contract(hidden, weighted, ((0,), (0,))).astype(jnp.bfloat16)
    return grad_gate, grad_up, grad_down, grad_input


def solution(mesh):
    fine = Mesh(mesh.devices.reshape(4, 4, 4, 2, 2, 2), ("y", "x", "zh", "zm", "zl", "c"))
    dp = ("y", "x", "zh")
    in_specs = (
        P(TENSOR, dp),
        P(TENSOR, dp),
        P(dp, TENSOR),
        P(dp, TENSOR),
        P(TENSOR, dp),
        P(TENSOR),
        P(TENSOR),
    )
    out_specs = (P(dp, TENSOR), P(dp, TENSOR), P(TENSOR, dp), P(TENSOR, dp))
    return jax.shard_map(shards, mesh=fine, in_specs=in_specs, out_specs=out_specs, check_vma=False)
```

```python
import jax
import jax.numpy as jnp
from jax import lax
from jax.experimental import pallas as pl
from jax.experimental.pallas import tpu as pltpu
from jax.sharding import Mesh, PartitionSpec as P

YX = ("x", "y")
TENSOR = ("zm", "zl", "c")
TOKENS = 384
FF = 1024


def contract(left, right, dims):
    return lax.dot_general(left, right, (dims, ((), ())), preferred_element_type=jnp.float32)


def token_scale(ids, weights):
    same = ids[:, None] == ids[None, :]
    total = jnp.sum(jnp.where(same, weights[None, :], 0.0), axis=1)
    count = jnp.sum(same.astype(jnp.float32), axis=1)
    return weights * count / total


def spread_kernel(partials, rest, out):
    for at in range(0, FF, 256):
        sums = []
        for kind in range(3):
            cut = slice(kind * FF + at, kind * FF + at + 256)
            total = rest[:, cut]
            for plane in range(4):
                total = total + partials[plane, :, cut].astype(jnp.float32)
            sums.append(total)
        gate, up, hidden_grad = sums
        sigma = jax.nn.sigmoid(gate)
        up_grad = hidden_grad * gate * sigma
        hidden = gate * sigma * up
        gate_grad = hidden_grad * up * sigma * (1.0 + gate * (1.0 - sigma))
        for kind, value in enumerate((hidden, gate_grad, up_grad)):
            value = value.astype(jnp.bfloat16)
            for copy in range(16):
                out[copy, :, kind * FF + at : kind * FF + at + 256] = value


def spread(partials, rest):
    vmem = pl.BlockSpec(memory_space=pltpu.VMEM)
    return pl.pallas_call(
        spread_kernel,
        out_shape=jax.ShapeDtypeStruct((16,) + rest.shape, jnp.bfloat16),
        in_specs=[vmem, vmem],
        out_specs=vmem,
        compiler_params=pltpu.CompilerParams(vmem_limit_bytes=16 * 1024 * 1024),
        name="spread",
    )(partials, rest)


def shards(inputs, out_grad, gate_weight, up_weight, down_weight, segment_ids, token_weights):
    token = lax.broadcasted_iota(jnp.int32, (TOKENS // 8, 128), 0)
    lane = lax.broadcasted_iota(jnp.int32, (TOKENS // 8, 128), 1)
    codes = jnp.pad(segment_ids, (0, 80)) + jnp.pad(token_weights, (64, 16))
    side = jnp.where((lane & 63) == token, codes[None, :], 0).astype(jnp.bfloat16)
    own = jnp.concatenate([inputs, out_grad, side], axis=1)
    every = lax.all_gather(own, TENSOR, axis=0, tiled=True)
    all_inputs, all_grads = every[:, :256], every[:, 256:512]
    sides = every[:, 512:].astype(jnp.float32)
    scale = token_scale(jnp.sum(sides[:, :64], axis=1), jnp.sum(sides[:, 64:], axis=1))
    weighted = (all_grads.astype(jnp.float32) * scale[:, None]).astype(jnp.bfloat16)

    parts = jnp.concatenate(
        [
            contract(all_inputs, gate_weight, ((1,), (0,))).astype(jnp.bfloat16),
            contract(all_inputs, up_weight, ((1,), (0,))).astype(jnp.bfloat16),
            contract(weighted, down_weight, ((1,), (1,))).astype(jnp.bfloat16),
        ],
        axis=1,
    )
    parts, weighted, all_inputs = lax.optimization_barrier((parts, weighted, all_inputs))
    pieces = lax.all_to_all(parts.reshape(16, TOKENS // 16, 3 * FF), YX, 0, 0)
    own_sum = jnp.sum(pieces.astype(jnp.float32), axis=0)
    rounded = lax.reduce_precision(own_sum, 8, 7)
    partials = lax.all_gather(rounded.astype(jnp.bfloat16), "zh", axis=0)
    blocks = lax.all_to_all(spread(partials, own_sum - rounded), YX, 0, 0)
    blocks = blocks.reshape(TOKENS, 3 * FF)
    hidden, gate_grad, up_grad = blocks[:, :FF], blocks[:, FF : 2 * FF], blocks[:, 2 * FF :]

    back = contract(gate_grad, gate_weight, ((1,), (1,))) + contract(up_grad, up_weight, ((1,), (1,)))
    back = back.astype(jnp.bfloat16).reshape(2, 2, 2, TOKENS // 8, 256).swapaxes(0, 1).reshape(8, TOKENS // 8, 256)
    back = lax.all_to_all(back, ("zl", "zm", "c"), 0, 0)
    grad_input = jnp.sum(back.astype(jnp.float32), axis=0).astype(jnp.bfloat16)
    grad_gate = contract(all_inputs, gate_grad, ((0,), (0,))).astype(jnp.bfloat16)
    grad_up = contract(all_inputs, up_grad, ((0,), (0,))).astype(jnp.bfloat16)
    grad_down = contract(hidden, weighted, ((0,), (0,))).astype(jnp.bfloat16)
    return grad_gate, grad_up, grad_down, grad_input


def solution(mesh):
    fine = Mesh(mesh.devices.reshape(4, 4, 4, 2, 2, 2), ("y", "x", "zh", "zm", "zl", "c"))
    dp = ("y", "x", "zh")
    in_specs = (
        P(TENSOR, dp),
        P(TENSOR, dp),
        P(dp, TENSOR),
        P(dp, TENSOR),
        P(TENSOR, dp),
        P(TENSOR),
        P(TENSOR),
    )
    out_specs = (P(dp, TENSOR), P(dp, TENSOR), P(TENSOR, dp), P(TENSOR, dp))
    return jax.shard_map(shards, mesh=fine, in_specs=in_specs, out_specs=out_specs, check_vma=False)
```
